32 devices in a mesh: frame: 16 (over z, x, core), band: 2 (over y).
Axes of the slice: x: 2, y: 2, z: 4, core: 2. Of those that a mesh axis runs over, the one named last changes fastest.
Arguments:
- frames: bfloat16 [128, 16, 16, 320], P('frame', 'band'), may hold values from -6 to 6
- control: bfloat16 [128, 16, 16, 320], P('frame', 'band'), may hold values from -4 to 4
- conv_first: bfloat16 [3, 3, 320, 320], replicated, may hold values from -0.109375 to 0.109375
- conv_second: bfloat16 [3, 3, 320, 320], replicated, may hold values from -0.109375 to 0.109375
- time_table: float32 [1000, 320], replicated, may hold values from -5 to 5
- step_index: int32 [1], replicated, may hold values from 0 to 999
- norm_gain: float32 [320], replicated, may hold values from 0.5 to 1.5
- w_query: bfloat16 [320, 320], replicated, as said below
- w_key: bfloat16 [320, 320], replicated, as said below
- w_value: bfloat16 [320, 320], replicated, may hold values from -0.3125 to 0.3125
- w_out: bfloat16 [320, 320], replicated, may hold values from -0.3125 to 0.3125
- rel_bias: float32 [8, 33], replicated, may hold values from -4 to 4
- reach: int32 [128], replicated, may hold values from 4 to 16, as said below
Outputs:
- section_out: float32 [128, 16, 16, 320], P('frame', 'band')
The draws below stay inside these ranges and needn't reach their ends.
Inputs may be any that keep to these rules, and one draw needn't show every extreme that they name: Each frame attends within reach[f] frames on the loop; the first and last frame of each aligned block of 8 frames have reach 16. `w_query`: projection into 8 heads. `w_key`: projection into 8 heads.
All inputs are finite; a program needn't handle non-finite values.
Results may differ from the reference program's by a relative error of at most 0.012.
The reference program's roundings to bfloat16 on the way (of `merged`, `activated`, `normed`, `weights` and `attended`) count: a program that leaves them out, or rounds other values in their place, can miss the bound.
Values may be sent and summed in bfloat16 or wider, within the bound.
A program may use at most 128 MiB of HBM per device.

```python
import jax
import jax.numpy as jnp
from jax import lax

C = 320
HEADS = 8
F_DEV = 8
COLS = 16
STEPS = 1000
REACH = 16
FRAMES = 128
ROWS = 16


def scaled_columns(key, spread):
    base = jax.random.normal(jax.random.fold_in(key, 1), (C, C), jnp.float32) * C ** (-0.5)
    factor = jnp.exp(jax.random.uniform(jax.random.fold_in(key, 2), (HEADS,), jnp.float32) * spread)
    return (base * jnp.repeat(factor, C // HEADS)[None, :]).astype(jnp.bfloat16)


def draw_w_query(key, part):
    key = jax.random.fold_in(key, 11)
    return scaled_columns(key, 0.0)


def draw_w_key(key, part):
    key = jax.random.fold_in(key, 12)
    return scaled_columns(key, 0.0)


def draw_reach(key, part):
    key = jax.random.fold_in(key, 13)
    base = jax.random.randint(key, (FRAMES,), 4, REACH + 1, dtype=jnp.int32)
    position = jnp.arange(FRAMES, dtype=jnp.int32) % F_DEV
    edge = (position == 0) | (position == F_DEV - 1)
    return jnp.where(edge, REACH, base).astype(jnp.int32)


def level_of(stream_key, extent, split, smallest, high):
    def one(axis_at, parts):
        heights = jax.random.uniform(jax.random.fold_in(jax.random.fold_in(stream_key, 6), axis_at), (parts,), jnp.float32, smallest / len(split), high / len(split))
        return jnp.repeat(jnp.exp(heights), extent[axis_at] // parts).reshape((-1,) + (1,) * (len(extent) - axis_at - 1))

    level = one(*split[0])
    for cut in split[1:]:
        level = level * one(*cut)
    return level


def scatter_about(rng, dims, scale, limit, pieces=(), kind=jnp.bfloat16):
    factor_of = level_of(rng, dims, pieces, -0.22, 0.18) if pieces else 1.0
    entries = jax.random.normal(rng, dims, jnp.float32) * scale * factor_of
    return jnp.minimum(jnp.maximum(entries, -limit), limit).astype(kind)


def setup_inputs(seed: int = 0) -> dict:
    arg_keys = jax.random.split(jax.random.key(seed), 14)
    frames = scatter_about(arg_keys[0], (FRAMES, ROWS, COLS, C), 1.0, 6.0, ((0, 16), (1, 2)))
    control = scatter_about(arg_keys[1], (FRAMES, ROWS, COLS, C), 0.5, 4.0, ((0, 16), (1, 2)))
    conv_first = scatter_about(arg_keys[2], (3, 3, C, C), (9 * C) ** -0.5, 0.109375)
    conv_second = scatter_about(arg_keys[3], (3, 3, C, C), (9 * C) ** -0.5, 0.109375)
    time_table = scatter_about(arg_keys[4], (STEPS, C), 1.0, 5.0, (), jnp.float32)
    step_index = jax.random.randint(arg_keys[5], (1,), 0, STEPS).astype(jnp.int32)
    norm_gain = jnp.clip(1.0 + 0.1 * jax.random.normal(arg_keys[6], (C,), jnp.float32), 0.5, 1.5)
    w_query = draw_w_query(jax.random.fold_in(arg_keys[13], 71), 0)
    w_key = draw_w_key(jax.random.fold_in(arg_keys[13], 71), 0)
    w_value = scatter_about(arg_keys[9], (C, C), C ** -0.5, 0.3125)
    w_out = scatter_about(arg_keys[10], (C, C), C ** -0.5, 0.3125)
    rel_bias = scatter_about(arg_keys[11], (HEADS, 2 * REACH + 1), 1.0, 4.0, (), jnp.float32)
    reach = draw_reach(jax.random.fold_in(arg_keys[13], 71), 0)
    return {"frames": frames, "control": control, "conv_first": conv_first, "conv_second": conv_second, "time_table": time_table, "step_index": step_index, "norm_gain": norm_gain, "w_query": w_query, "w_key": w_key, "w_value": w_value, "w_out": w_out, "rel_bias": rel_bias, "reach": reach}


def conv_full(field, weight):
    return lax.conv_general_dilated(field.astype(jnp.float32), weight.astype(jnp.float32), (1, 1), ((1, 1), (1, 1)), dimension_numbers=('NHWC', 'HWIO', 'NHWC'), precision=lax.Precision.HIGHEST)

def attend(query, key, value, q_frames, k_frames, reach_q, rel_bias, total):
    heads = rel_bias.shape[0]
    span = (rel_bias.shape[1] - 1) // 2
    fq, pix, chans = query.shape
    fk = key.shape[0]
    dh = chans // heads
    q4 = query.reshape(fq, pix, heads, dh).astype(jnp.float32)
    k4 = key.reshape(fk, pix, heads, dh).astype(jnp.float32)
    v4 = value.reshape(fk, pix, heads, dh).astype(jnp.float32)
    scores = jnp.einsum('iphd,jphd->phij', q4, k4) * dh ** (-0.5)
    delta = ((k_frames[None, :] - q_frames[:, None] + total // 2) % total - total // 2).astype(jnp.int32)
    table = (delta[:, :, None] + span == jnp.arange(2 * span + 1, dtype=jnp.int32)[None, None, :]).astype(jnp.float32)
    bias = jnp.einsum('ijs,hs->hij', table, rel_bias, precision=lax.Precision.HIGHEST)
    allowed = jnp.abs(delta) <= reach_q[:, None]
    scores = jnp.where(allowed[None, None], scores + bias[None], -jnp.inf)
    top = lax.optimization_barrier(jnp.max(scores, axis=-1, keepdims=True))
    expo = jnp.exp(scores - top)
    weights = (expo / lax.optimization_barrier(jnp.sum(expo, axis=-1, keepdims=True))).astype(jnp.bfloat16)
    out = jnp.einsum('phij,jphd->iphd', weights.astype(jnp.float32), v4)
    return out.astype(jnp.bfloat16).reshape(fq, pix, chans)

def reference(frames, control, conv_first, conv_second, time_table, step_index, norm_gain, w_query, w_key, w_value, w_out, rel_bias, reach):
    total, rows, cols, chans = frames.shape
    pixels = rows * cols
    blocks = total // F_DEV
    picker = (jnp.arange(time_table.shape[0], dtype=jnp.int32) == step_index[0]).astype(jnp.float32)
    embed = jnp.dot(picker, time_table, precision=lax.Precision.HIGHEST)

    def front(pair):
        xin, cin = pair
        merged = (xin.astype(jnp.float32) + cin.astype(jnp.float32)).astype(jnp.bfloat16)
        activated = jax.nn.silu(conv_full(merged, conv_first) + embed).astype(jnp.bfloat16)
        block_out = merged.astype(jnp.float32) + conv_full(activated, conv_second)
        flat = block_out.reshape(F_DEV * pixels, chans)
        centre = flat - lax.optimization_barrier(jnp.mean(flat, axis=1, keepdims=True))
        normed = (centre * lax.rsqrt(lax.optimization_barrier(jnp.mean(centre * centre, axis=1, keepdims=True)) + 1e-05) * norm_gain).astype(jnp.bfloat16)
        query = jnp.dot(normed, w_query, preferred_element_type=jnp.float32).astype(jnp.bfloat16)
        key = jnp.dot(normed, w_key, preferred_element_type=jnp.float32).astype(jnp.bfloat16)
        value = jnp.dot(normed, w_value, preferred_element_type=jnp.float32).astype(jnp.bfloat16)
        return (flat.reshape(F_DEV, pixels, chans), query.reshape(F_DEV, pixels, chans), key.reshape(F_DEV, pixels, chans), value.reshape(F_DEV, pixels, chans))
    shaped = (frames.reshape(blocks, F_DEV, rows, cols, chans), control.reshape(blocks, F_DEV, rows, cols, chans))
    block_out, query, key, value = lax.map(front, shaped)
    key = key.reshape(total, pixels, chans)
    value = value.reshape(total, pixels, chans)
    hops = -(-REACH // F_DEV)

    def back(item):
        index, q_blk, r_blk = item
        base = index * F_DEV
        picks = ((base + jnp.arange(-hops * F_DEV, (hops + 1) * F_DEV, dtype=jnp.int32)) % total).astype(jnp.int32)
        q_frames = (base + jnp.arange(F_DEV, dtype=jnp.int32)).astype(jnp.int32)
        reach_q = lax.dynamic_slice_in_dim(reach, base.astype(jnp.int32), F_DEV)
        attended = attend(q_blk, jnp.take(key, picks, axis=0), jnp.take(value, picks, axis=0), q_frames, picks, reach_q, rel_bias, total)
        mixed = jnp.dot(attended.reshape(F_DEV * pixels, chans), w_out, preferred_element_type=jnp.float32)
        return r_blk.reshape(F_DEV * pixels, chans) + mixed
    result = lax.map(back, (jnp.arange(blocks, dtype=jnp.int32), query, block_out))
    return result.reshape(total, rows, cols, chans)
```

```python
import functools

import jax
import jax.numpy as jnp
import numpy as np
from jax import lax
from jax.experimental import pallas as pl
from jax.experimental.pallas import tpu as pltpu
from jax.sharding import PartitionSpec as P

MESH = pl.DeviceIdType.MESH
LOG2E = 1.4426950408889634
GROUP = 4
BF16 = jnp.bfloat16
F32 = jnp.float32


def taps(flat, cols):
    n = flat.shape[0]
    col = lax.broadcasted_iota(jnp.int32, flat.shape, 0) % cols
    left = jnp.where(col == 0, 0.0, pltpu.roll(flat, 1, 0))
    right = jnp.where(col == cols - 1, 0.0, pltpu.roll(flat, n - 1, 0))
    return jnp.concatenate([left.astype(BF16), flat.astype(BF16), right.astype(BF16)], axis=-1)


def front_kernel(
    nb, step,
    x_ref, c_ref, w1_ref, w2_ref, embed_ref, gain_ref, perm_ref,
    bo_ref, normed_ref,
    mpad, top, bottom, wide1, wide2, nf, send_sem, recv_sem,
):
    count, rows, cols, chans = x_ref.shape
    me = lax.axis_index("band")
    up, down = (me + nb - 1) % nb, (me + 1) % nb
    barrier = pltpu.get_barrier_semaphore()
    for other in (up, down):
        pl.semaphore_signal(barrier, inc=1, device_id={"band": other}, device_id_type=MESH)
    mpad[:, 2 : 2 + rows] = (x_ref[...].astype(F32) + c_ref[...].astype(F32)).astype(BF16)
    pl.semaphore_wait(barrier, 2)
    to_down = pltpu.make_async_remote_copy(
        src_ref=mpad.at[:, pl.ds(rows, 2)], dst_ref=top, send_sem=send_sem.at[0],
        recv_sem=recv_sem.at[0], device_id={"band": down}, device_id_type=MESH,
    )
    to_up = pltpu.make_async_remote_copy(
        src_ref=mpad.at[:, pl.ds(2, 2)], dst_ref=bottom, send_sem=send_sem.at[1],
        recv_sem=recv_sem.at[1], device_id={"band": up}, device_id_type=MESH,
    )
    to_down.start()
    to_up.start()
    to_down.wait()
    to_up.wait()
    has_top = (me > 0).astype(F32)
    has_bottom = (me < nb - 1).astype(F32)
    mpad[:, 0:2] = (top[...].astype(F32) * has_top).astype(BF16)
    mpad[:, 2 + rows : 4 + rows] = (bottom[...].astype(F32) * has_bottom).astype(BF16)

    def frames_step(i, carry):
        at = pl.ds(i * step, step)
        flat = mpad[at].reshape(step * (rows + 4) * cols, chans).astype(F32)
        wide1[...] = taps(flat, cols).reshape(wide1.shape)
        acc = embed_ref[...]
        for a in range(3):
            acc = acc + jnp.dot(
                wide1[:, a : a + rows + 2].reshape(step * (rows + 2) * cols, 3 * chans),
                w1_ref[a], preferred_element_type=F32,
            )
        act = acc / (1.0 + jnp.exp(-acc))
        row = (lax.broadcasted_iota(jnp.int32, act.shape, 0) // cols) % (rows + 2)
        inside = jnp.where(row == 0, has_top, jnp.where(row == rows + 1, has_bottom, 1.0))
        act = act * inside
        wide2[...] = taps(act, cols).reshape(wide2.shape)
        out = mpad[at, 2 : 2 + rows].reshape(step * rows * cols, chans).astype(F32)
        conv = None
        for a in range(3):
            part = jnp.dot(
                wide2[:, a : a + rows].reshape(step * rows * cols, 3 * chans),
                w2_ref[a], preferred_element_type=F32,
            )
            conv = part if conv is None else conv + part
        out = out + conv
        bo_ref[at] = out.reshape(step, rows, cols, chans)
        centre = out - jnp.mean(out, axis=1, keepdims=True)
        scale = lax.rsqrt(jnp.mean(centre * centre, axis=1, keepdims=True) + 1e-05)
        nf[at] = (centre * scale * gain_ref[...]).astype(BF16).reshape(step, rows, cols, chans)
        return carry

    lax.fori_loop(0, count // step, frames_step, 0)
    for y in range(rows):
        block = nf[:, y].reshape(count * cols, chans)
        normed_ref[y * count * cols : (y + 1) * count * cols] = jnp.dot(
            perm_ref[...], block, preferred_element_type=F32
        ).astype(BF16)


def back_kernel(
    n, heads, scale,
    normed_ref, bo_ref, wq_ref, wkv_ref, wo_ref, bias_ref, head_ref, perm_ref,
    out_ref,
    win, qbuf, kbuf, vbuf, att, got,
    send_a, recv_a, send_b, recv_b, send_d, recv_d,
):
    count, rows, cols, chans = bo_ref.shape
    part = win.shape[1]
    me = lax.axis_index("frame")
    r = me % GROUP
    base = me - r
    after, before = (me + GROUP) % n, (me + n - GROUP) % n
    mates = [base + (r + d) % GROUP for d in range(1, GROUP)]
    barrier = pltpu.get_barrier_semaphore()
    for other in mates + [after, before]:
        pl.semaphore_signal(barrier, inc=1, device_id={"frame": other}, device_id_type=MESH)
    pl.semaphore_wait(barrier, GROUP + 1)

    def quarter(j):
        return pl.ds(pl.multiple_of(j * part, part), part)

    def to_mate(j):
        return pltpu.make_async_remote_copy(
            src_ref=normed_ref.at[quarter(j)], dst_ref=win.at[2 + r], send_sem=send_a.at[j],
            recv_sem=recv_a.at[r], device_id={"frame": base + j}, device_id_type=MESH,
        )

    def from_mate(j):
        return pltpu.make_async_remote_copy(
            src_ref=normed_ref.at[quarter(j)], dst_ref=win.at[2 + j], send_sem=send_a.at[j],
            recv_sem=recv_a.at[j], device_id={"frame": base + j}, device_id_type=MESH,
        )

    def along(j):
        return pltpu.make_async_remote_copy(
            src_ref=win.at[2 + j], dst_ref=win.at[(j + 6) % 8], send_sem=send_b.at[j],
            recv_sem=recv_b.at[j], device_id={"frame": (me + GROUP * (2 * (j // 2) - 1) + n) % n},
            device_id_type=MESH,
        )

    def back_to(j):
        return pltpu.make_async_remote_copy(
            src_ref=att.at[j], dst_ref=got.at[r], send_sem=send_d.at[j],
            recv_sem=recv_d.at[r], device_id={"frame": base + j}, device_id_type=MESH,
        )

    def back_from(j):
        return pltpu.make_async_remote_copy(
            src_ref=att.at[j], dst_ref=got.at[j], send_sem=send_d.at[j],
            recv_sem=recv_d.at[j], device_id={"frame": base + j}, device_id_type=MESH,
        )

    others = [(r + d) % GROUP for d in range(1, GROUP)]
    for j in others:
        to_mate(j).start()
    win[2 + r] = normed_ref[quarter(r)]
    along(r).start()
    for j in others:
        from_mate(j).wait_recv()
        along(j).start()

    def project(slot):
        kv = jnp.dot(win[slot], wkv_ref[...], preferred_element_type=F32).astype(BF16)
        kbuf[slot] = kv[:, :chans]
        vbuf[slot] = kv[:, chans:]

    for j in range(GROUP):
        project(2 + j)
        qbuf[j] = jnp.dot(win[2 + j], wq_ref[...], preferred_element_type=F32).astype(BF16)
    for j in range(GROUP):
        to = (j + 6) % 8
        pltpu.make_async_remote_copy(
            src_ref=win.at[2 + j], dst_ref=win.at[to], send_sem=send_b.at[j],
            recv_sem=recv_b.at[j], device_id={"frame": after}, device_id_type=MESH,
        ).wait_recv()
        project(to)

    def pair(i, carry):
        at = pl.ds(pl.multiple_of(i * 16, 16), 16)
        q = qbuf[:, at].reshape(GROUP * 16, chans)
        k = kbuf[:, at].reshape(128, chans)
        v = vbuf[:, at].reshape(128, chans)
        qx = jnp.concatenate([q * head_ref[h] for h in range(heads)], axis=0)
        s = lax.dot_general(qx, k, (((1,), (1,)), ((), ())), preferred_element_type=F32)
        s = s * scale + bias_ref[...]
        e = jnp.exp2(s - jnp.max(s, axis=1, keepdims=True))
        w = (e * (1.0 / jnp.sum(e, axis=1, keepdims=True))).astype(BF16)
        w = jnp.concatenate([w[h * 64 : (h + 1) * 64] for h in range(heads)], axis=1)
        vx = jnp.concatenate([v * head_ref[h] for h in range(heads)], axis=0)
        o = jnp.dot(w, vx, preferred_element_type=F32).astype(BF16)
        att[:, at] = o.reshape(GROUP, 16, chans)
        return carry

    lax.fori_loop(0, part // 16, pair, 0)
    for j in others:
        back_to(j).start()
    got[r] = att[r]
    for j in others:
        back_from(j).wait_recv()
    for y in range(rows):
        size = count * cols
        first = y * size
        block = got[first // part, first % part : first % part + size]
        block = jnp.dot(perm_ref[...], block, preferred_element_type=F32).astype(BF16)
        mixed = jnp.dot(block, wo_ref[...], preferred_element_type=F32)
        out_ref[:, y] = bo_ref[:, y] + mixed.reshape(count, cols, chans)
    for j in others:
        to_mate(j).wait_send()
        back_to(j).wait_send()
    for j in range(GROUP):
        along(j).wait_send()


def bias_table(rel_bias, reach_group, count):
    heads, width = rel_bias.shape
    span = (width - 1) // 2
    q = np.arange(GROUP * 2 * count)
    k = np.arange((GROUP + 4) * 2 * count)
    q_frame = q // (2 * count) * count + q % count
    k_frame = k // (2 * count) * count + k % count - 2 * count
    delta = k_frame[None, :] - q_frame[:, None]
    same = (q // count % 2)[:, None] == (k // count % 2)[None, :]
    delta_j = jnp.asarray(delta, jnp.int32)
    reach_rows = jnp.broadcast_to(
        reach_group.reshape(GROUP, 1, count), (GROUP, 2, count)
    ).reshape(-1, 1)
    allowed = jnp.logical_and(jnp.abs(delta_j) <= reach_rows, jnp.asarray(same))
    table = (delta_j[None] + span == jnp.arange(width, dtype=jnp.int32)[:, None, None]).astype(F32)
    bias = jnp.einsum("hs,sij->hij", rel_bias * LOG2E, table, precision=lax.Precision.HIGHEST)
    return jnp.where(allowed[None], bias, -jnp.inf).reshape(heads * q.size, k.size)


def shards(
    n, nb,
    frames, control, conv_first, conv_second, time_table, step_index, norm_gain,
    w_query, w_key, w_value, w_out, rel_bias, reach,
):
    count, rows, cols, chans = frames.shape
    heads = rel_bias.shape[0]
    pixels = rows * cols
    part = count * pixels // GROUP
    embed = lax.dynamic_slice_in_dim(time_table, step_index[0], 1, axis=0)
    perm = np.zeros((count * cols, count * cols), np.float32)
    for f in range(count):
        for x in range(cols):
            perm[x * count + f, f * cols + x] = 1.0
    to_pixels = jnp.asarray(perm, BF16)
    to_frames = jnp.asarray(perm.T, BF16)
    head_of = np.arange(chans) // (chans // heads)
    head_mask = jnp.asarray(
        (head_of[None, None, :] == np.arange(heads)[:, None, None]).astype(np.float32), BF16
    )
    vmem = pl.BlockSpec(memory_space=pltpu.VMEM)
    step = 4
    block_out, normed = pl.pallas_call(
        functools.partial(front_kernel, nb, step),
        out_shape=(
            jax.ShapeDtypeStruct((count, rows, cols, chans), F32),
            jax.ShapeDtypeStruct((count * pixels, chans), BF16),
        ),
        in_specs=[vmem] * 7,
        out_specs=(vmem, vmem),
        scratch_shapes=[
            pltpu.VMEM((count, rows + 4, cols, chans), BF16),
            pltpu.VMEM((count, 2, cols, chans), BF16),
            pltpu.VMEM((count, 2, cols, chans), BF16),
            pltpu.VMEM((step, rows + 4, cols, 3 * chans), BF16),
            pltpu.VMEM((step, rows + 2, cols, 3 * chans), BF16),
            pltpu.VMEM((count, rows, cols, chans), BF16),
            pltpu.SemaphoreType.DMA((2,)),
            pltpu.SemaphoreType.DMA((2,)),
        ],
        compiler_params=pltpu.CompilerParams(
            collective_id=0, has_side_effects=True, vmem_limit_bytes=48 * 2**20
        ),
    )(
        frames, control, conv_first.reshape(3, 3 * chans, chans),
        conv_second.reshape(3, 3 * chans, chans), embed, norm_gain.reshape(1, chans), to_pixels,
    )
    start = lax.axis_index("frame") // GROUP * (GROUP * count)
    bias = bias_table(rel_bias, lax.dynamic_slice_in_dim(reach, start, GROUP * count), count)
    dma = pltpu.SemaphoreType.DMA((GROUP,))
    window = GROUP + 4
    out = pl.pallas_call(
        functools.partial(back_kernel, n, heads, LOG2E * (chans // heads) ** (-0.5)),
        out_shape=jax.ShapeDtypeStruct((count, rows, cols, chans), F32),
        in_specs=[vmem] * 8,
        out_specs=vmem,
        scratch_shapes=[
            pltpu.VMEM((window, part, chans), BF16),
            pltpu.VMEM((GROUP, part, chans), BF16),
            pltpu.VMEM((window, part, chans), BF16),
            pltpu.VMEM((window, part, chans), BF16),
            pltpu.VMEM((GROUP, part, chans), BF16),
            pltpu.VMEM((GROUP, part, chans), BF16),
            dma, dma, dma, dma, dma, dma,
        ],
        compiler_params=pltpu.CompilerParams(
            collective_id=1, has_side_effects=True, vmem_limit_bytes=48 * 2**20
        ),
    )(
        normed, block_out, w_query, jnp.concatenate([w_key, w_value], axis=1), w_out, bias,
        head_mask, to_frames,
    )
    return out


def solution(mesh):
    split = P("frame", "band", None, None)
    return jax.shard_map(
        functools.partial(shards, mesh.shape["frame"], mesh.shape["band"]),
        mesh=mesh,
        in_specs=(split, split) + (P(),) * 11,
        out_specs=split,
        check_vma=False,
    )
```

```python
import functools

import jax
import jax.numpy as jnp
from jax import lax
from jax.experimental import pallas as pl
from jax.experimental.pallas import tpu as pltpu
from jax.sharding import PartitionSpec as P

MESH = pl.DeviceIdType.MESH
LOG2E = 1.4426950408889634
GROUP = 4
BF16 = jnp.bfloat16
F32 = jnp.float32


def taps(flat, cols):
    n = flat.shape[0]
    col = lax.broadcasted_iota(jnp.int32, flat.shape, 0) % cols
    left = jnp.where(col == 0, 0.0, pltpu.roll(flat, 1, 0))
    right = jnp.where(col == cols - 1, 0.0, pltpu.roll(flat, n - 1, 0))
    return jnp.concatenate([left.astype(BF16), flat.astype(BF16), right.astype(BF16)], axis=-1)


def kernel(
    n, nb, heads, span,
    x_hbm, c_hbm, w1_hbm, w2_hbm, table_hbm, wq_hbm, wk_hbm, wv_hbm, wo_hbm,
    step_ref, rel_ref, gain_ref, reach_ref,
    out_ref,
    x_ref, c_ref, w1_ref, w2_ref, table_ref, wq_ref, wk_ref, wv_ref, wo_ref,
    merged, top, bottom, wide1, wide2, block_out, ready, win, att, got, bias, load_sem,
    send_h, recv_h, send_a, recv_a, send_b, recv_b, send_d, recv_d,
):
    count, rows, cols, chans = x_ref.shape
    chunks = rows // 2
    quart = cols // GROUP
    part = 2 * quart * count
    size = GROUP * part
    slots = GROUP + 4
    me, mb = lax.axis_index("frame"), lax.axis_index("band")
    up, down = (mb + nb - 1) % nb, (mb + 1) % nb
    r = me % GROUP
    base = me - r
    after, before = (me + GROUP) % n, (me + n - GROUP) % n
    others = [(r + d) % GROUP for d in range(1, GROUP)]

    barrier = pltpu.get_barrier_semaphore()
    for other in (up, down):
        pl.semaphore_signal(barrier, inc=1, device_id={"band": other}, device_id_type=MESH)
    for other in [base + j for j in others] + [after, before]:
        pl.semaphore_signal(barrier, inc=1, device_id={"frame": other}, device_id_type=MESH)
    pairs = [
        (x_hbm, x_ref), (c_hbm, c_ref), (w1_hbm, w1_ref), (table_hbm, table_ref), (w2_hbm, w2_ref),
        (wq_hbm, wq_ref), (wk_hbm, wk_ref), (wv_hbm, wv_ref), (wo_hbm, wo_ref),
    ]
    loads = [pltpu.make_async_copy(s, d, load_sem.at[i]) for i, (s, d) in enumerate(pairs)]
    for load in loads:
        load.start()

    def halo(src, dst, i, other):
        return pltpu.make_async_remote_copy(
            src_ref=src, dst_ref=dst, send_sem=send_h.at[i], recv_sem=recv_h.at[i],
            device_id={"band": other}, device_id_type=MESH,
        )

    def share(j):
        return pl.ds(pl.multiple_of(j * part, part), part)

    def to_mate(k, j, slot, sem):
        return pltpu.make_async_remote_copy(
            src_ref=ready.at[k, share(j)], dst_ref=win.at[k, 2 + slot], send_sem=send_a.at[k, j],
            recv_sem=recv_a.at[k, sem], device_id={"frame": base + j}, device_id_type=MESH,
        )

    def along(k, j):
        return pltpu.make_async_remote_copy(
            src_ref=win.at[k, 2 + j], dst_ref=win.at[k, (j + 6) % 8], send_sem=send_b.at[k, j],
            recv_sem=recv_b.at[k, j], device_id={"frame": (me + GROUP * (2 * (j // 2) - 1) + n) % n},
            device_id_type=MESH,
        )

    def back_to(k, j, place, sem):
        return pltpu.make_async_remote_copy(
            src_ref=att.at[k, j], dst_ref=got.at[k, place], send_sem=send_d.at[k, j],
            recv_sem=recv_d.at[k, sem], device_id={"frame": base + j}, device_id_type=MESH,
        )

    loads[0].wait()
    loads[1].wait()
    merged[...] = (x_ref[...].astype(F32) + c_ref[...].astype(F32)).astype(BF16)
    pl.semaphore_wait(barrier, GROUP + 3)
    to_down = halo(merged.at[:, pl.ds(rows - 2, 2)], top, 0, down)
    to_up = halo(merged.at[:, pl.ds(0, 2)], bottom, 1, up)
    to_down.start()
    to_up.start()

    def widen(at, block):
        flat = block.astype(F32).reshape(-1, chans)
        wide1[:, at : at + block.shape[1]] = taps(flat, cols).reshape(block.shape[:3] + (3 * chans,))

    for y in range(0, rows, 2):
        widen(2 + y, merged[:, y : y + 2])

    steps = table_ref.shape[1]
    picked = (lax.broadcasted_iota(jnp.int32, (8, steps), 1) == step_ref[0]).astype(F32)
    loads[3].wait()
    embed = lax.dot_general(
        picked, table_ref[...], (((1,), (1,)), ((), ())),
        precision=lax.Precision.HIGHEST, preferred_element_type=F32,
    )[0:1]
    to = lax.broadcasted_iota(jnp.int32, (size, size), 0)
    of = lax.broadcasted_iota(jnp.int32, (size, size), 1)

    def source(i):
        quarter, y = i // part, (i // (quart * count)) % 2
        return (i % count) * (2 * cols) + y * cols + quarter * quart + (i // count) % quart

    to_pixels = (source(to) == of).astype(F32).astype(BF16)
    to_frames = (source(of) == to).astype(F32).astype(BF16)
    has_top = (mb > 0).astype(F32)
    has_bottom = (mb < nb - 1).astype(F32)
    loads[2].wait()

    def first_conv(m):
        acc = embed
        for a in range(3):
            acc = acc + jnp.dot(
                wide1[:, 2 * m + a : 2 * m + a + 2].reshape(size, 3 * chans), w1_ref[a],
                preferred_element_type=F32,
            )
        act = acc / (1.0 + jnp.exp(-acc))
        row = (lax.broadcasted_iota(jnp.int32, act.shape, 0) // cols) % 2
        if m == 0:
            act = act * jnp.where(row == 0, has_top, 1.0)
        if m == chunks:
            act = act * jnp.where(row == 1, has_bottom, 1.0)
        wide2[:, 2 * m : 2 * m + 2] = taps(act, cols).reshape(count, 2, cols, 3 * chans)

    def second_conv(j, k):
        out = merged[:, 2 * j : 2 * j + 2].reshape(size, chans).astype(F32)
        conv = None
        for a in range(3):
            part_sum = jnp.dot(
                wide2[:, 2 * j + a : 2 * j + a + 2].reshape(size, 3 * chans), w2_ref[a],
                preferred_element_type=F32,
            )
            conv = part_sum if conv is None else conv + part_sum
        out = out + conv
        block_out[:, 2 * j : 2 * j + 2] = out.reshape(count, 2, cols, chans)
        centre = out - jnp.mean(out, axis=1, keepdims=True)
        scale = lax.rsqrt(jnp.mean(centre * centre, axis=1, keepdims=True) + 1e-05)
        normed = (centre * scale * gain_ref[...].reshape(1, chans)).astype(BF16)
        ready[k] = jnp.dot(to_pixels, normed, preferred_element_type=F32).astype(BF16)
        for i in others:
            to_mate(k, i, r, r).start()
        win[k, 2 + r] = ready[k, share(r)]
        along(k, r).start()

    def forward(k):
        for i in others:
            to_mate(k, i, i, i).wait_recv()
            along(k, i).start()

    order = list(range(1, chunks - 1)) + [0, chunks - 1]
    first_conv(1)
    for k, j in enumerate(order):
        if j == 0:
            to_down.wait()
            to_up.wait()
            widen(0, top[...].astype(F32) * has_top)
            widen(2 + rows, bottom[...].astype(F32) * has_bottom)
            first_conv(0)
        else:
            first_conv(j + 1)
        if k == 0:
            loads[4].wait()
        second_conv(j, k)
        if k > 0:
            forward(k - 1)

    q = lax.broadcasted_iota(jnp.int32, (GROUP * 2 * count, slots * 2 * count), 0)
    c = lax.broadcasted_iota(jnp.int32, (GROUP * 2 * count, slots * 2 * count), 1)
    q_frame = q // (2 * count) * count + q % count
    delta = c // (2 * count) * count + c % count - 2 * count - q_frame
    total = reach_ref.shape[0]
    lane = lax.broadcasted_iota(jnp.int32, (q.shape[0], total), 1)
    q_of = lax.broadcasted_iota(jnp.int32, (q.shape[0], total), 0)
    q_of = q_of // (2 * count) * count + q_of % count + base * count
    limit = jnp.sum(
        jnp.where(lane == q_of, reach_ref[...].reshape(1, total).astype(F32), 0.0),
        axis=1, keepdims=True,
    )
    same = (q // count) % 2 == (c // count) % 2
    allowed = jnp.logical_and(jnp.abs(delta).astype(F32) <= limit, same)
    tables = [jnp.zeros(q.shape, F32) for _ in range(heads)]
    for s in range(2 * span + 1):
        hit = delta == s - span
        for h in range(heads):
            tables[h] = jnp.where(hit, rel_ref[h, s], tables[h])
    for h in range(heads):
        bias[h * q.shape[0] : (h + 1) * q.shape[0]] = jnp.where(
            allowed, tables[h] * LOG2E, -jnp.inf
        )
    forward(chunks - 1)

    for load in loads[5:]:
        load.wait()
    head_of = lax.broadcasted_iota(jnp.int32, (1, chans), 1) // (chans // heads)
    masks = [(head_of == h).astype(F32).astype(BF16) for h in range(heads)]
    scale = LOG2E * (chans // heads) ** (-0.5)
    edge = GROUP * 2 * count

    def attend(k, carry):
        for j in range(GROUP):
            along(k, j).wait_recv()
        field = win[k].reshape(slots * part, chans)
        keys = jnp.dot(field, wk_ref[...], preferred_element_type=F32)
        values = jnp.dot(field, wv_ref[...], preferred_element_type=F32)
        queries = jnp.dot(
            field[2 * part : (2 + GROUP) * part], wq_ref[...], preferred_element_type=F32
        )
        keys = keys.astype(BF16).reshape(slots, part, chans)
        values = values.astype(BF16).reshape(slots, part, chans)
        queries = queries.astype(BF16).reshape(GROUP, part, chans)
        for first in range(0, part, 2 * count):
            last = first + 2 * count
            qs = queries[:, first:last].reshape(edge, chans)
            ks = keys[:, first:last].reshape(slots * 2 * count, chans)
            vs = values[:, first:last].reshape(slots * 2 * count, chans)
            qx = jnp.concatenate([qs * mask for mask in masks], axis=0)
            s = lax.dot_general(qx, ks, (((1,), (1,)), ((), ())), preferred_element_type=F32)
            s = s * scale + bias[...]
            e = jnp.exp2(s - jnp.max(s, axis=1, keepdims=True))
            w = (e * (1.0 / jnp.sum(e, axis=1, keepdims=True))).astype(BF16)
            w = jnp.concatenate([w[h * edge : (h + 1) * edge] for h in range(heads)], axis=1)
            vx = jnp.concatenate([vs * mask for mask in masks], axis=0)
            o = jnp.dot(w, vx, preferred_element_type=F32).astype(BF16)
            att[k, :, first:last] = o.reshape(GROUP, 2 * count, chans)
        for j in others:
            back_to(k, j, r, r).start()
        got[k, r] = att[k, r]
        return carry

    lax.fori_loop(0, chunks, attend, 0)
    for k, y in enumerate(order):
        for j in others:
            back_to(k, j, j, j).wait_recv()
        block = got[k].reshape(size, chans)
        block = jnp.dot(to_frames, block, preferred_element_type=F32).astype(BF16)
        mixed = jnp.dot(block, wo_ref[...], preferred_element_type=F32)
        out_ref[:, 2 * y : 2 * y + 2] = block_out[:, 2 * y : 2 * y + 2] + mixed.reshape(
            count, 2, cols, chans
        )
    for k in range(chunks):
        for j in others:
            to_mate(k, j, r, r).wait_send()
            back_to(k, j, r, r).wait_send()
        for j in range(GROUP):
            along(k, j).wait_send()


def shards(
    n, nb,
    frames, control, conv_first, conv_second, time_table, step_index, norm_gain,
    w_query, w_key, w_value, w_out, rel_bias, reach,
):
    count, rows, cols, chans = frames.shape
    heads, width = rel_bias.shape
    chunks, part, slots = rows // 2, 2 * cols // GROUP * count, GROUP + 4
    table = time_table.T
    hbm = pl.BlockSpec(memory_space=pltpu.HBM)
    smem = pl.BlockSpec(memory_space=pltpu.SMEM)
    vmem = pl.BlockSpec(memory_space=pltpu.VMEM)
    wide = (3, 3 * chans, chans)
    square = pltpu.VMEM((chans, chans), BF16)
    dma = pltpu.SemaphoreType.DMA((chunks, GROUP))
    return pl.pallas_call(
        functools.partial(kernel, n, nb, heads, (width - 1) // 2),
        out_shape=jax.ShapeDtypeStruct((count, rows, cols, chans), F32),
        in_specs=[hbm] * 9 + [smem, smem, vmem, vmem],
        out_specs=vmem,
        scratch_shapes=[
            pltpu.VMEM(frames.shape, BF16),
            pltpu.VMEM(frames.shape, BF16),
            pltpu.VMEM(wide, BF16),
            pltpu.VMEM(wide, BF16),
            pltpu.VMEM(table.shape, F32),
            square, square, square, square,
            pltpu.VMEM(frames.shape, BF16),
            pltpu.VMEM((count, 2, cols, chans), BF16),
            pltpu.VMEM((count, 2, cols, chans), BF16),
            pltpu.VMEM((count, rows + 4, cols, 3 * chans), BF16),
            pltpu.VMEM((count, rows + 2, cols, 3 * chans), BF16),
            pltpu.VMEM(frames.shape, F32),
            pltpu.VMEM((chunks, GROUP * part, chans), BF16),
            pltpu.VMEM((chunks, slots, part, chans), BF16),
            pltpu.VMEM((chunks, GROUP, part, chans), BF16),
            pltpu.VMEM((chunks, GROUP, part, chans), BF16),
            pltpu.VMEM((heads * GROUP * 2 * count, slots * 2 * count), F32),
            pltpu.SemaphoreType.DMA((9,)),
            pltpu.SemaphoreType.DMA((2,)),
            pltpu.SemaphoreType.DMA((2,)),
            dma, dma, dma, dma, dma, dma,
        ],
        compiler_params=pltpu.CompilerParams(
            collective_id=0, has_side_effects=True, vmem_limit_bytes=56 * 2**20
        ),
    )(
        frames, control, conv_first.reshape(wide), conv_second.reshape(wide), table,
        w_query, w_key, w_value, w_out, step_index, rel_bias, norm_gain, reach,
    )


def solution(mesh):
    split = P("frame", "band", None, None)
    return jax.shard_map(
        functools.partial(shards, mesh.shape["frame"], mesh.shape["band"]),
        mesh=mesh,
        in_specs=(split, split) + (P(),) * 11,
        out_specs=split,
        check_vma=False,
    )
```

```python
import functools

import jax
import jax.numpy as jnp
from jax import lax
from jax.experimental import pallas as pl
from jax.experimental.pallas import tpu as pltpu
from jax.sharding import PartitionSpec as P

MESH = pl.DeviceIdType.MESH
LOG2E = 1.4426950408889634
GROUP = 4
BF16 = jnp.bfloat16
F32 = jnp.float32


def taps(block):
    shape = block.shape
    cols, chans = shape[2:]
    flat = block.astype(F32).reshape(-1, chans)
    n = flat.shape[0]
    col = lax.broadcasted_iota(jnp.int32, (1, cols, chans), 1)
    left = pltpu.roll(flat, 1, 0).reshape(-1, cols, chans) * (col > 0).astype(F32)
    right = pltpu.roll(flat, n - 1, 0).reshape(-1, cols, chans) * (col < cols - 1).astype(F32)
    sides = [left.astype(BF16), flat.astype(BF16).reshape(-1, cols, chans), right.astype(BF16)]
    return jnp.concatenate(sides, axis=-1).reshape(shape[:3] + (3 * chans,))


def kernel(
    n, nb, heads, span,
    x_hbm, c_hbm, w1_hbm, w2_hbm, table_hbm, wq_hbm, wk_hbm, wv_hbm, wo_hbm,
    step_ref, rel_ref, gain_ref, reach_ref,
    out_ref,
    x_ref, c_ref, w1_ref, w2_ref, table_ref, wq_ref, wk_ref, wv_ref, wo_ref,
    merged, top, bottom, wide1, wide2, block_out, ready, win, att, got, bias, load_sem,
    send_h, recv_h, send_a, recv_a, send_b, recv_b, send_d, recv_d,
):
    count, rows, cols, chans = x_ref.shape
    chunks = rows // 2
    quart = cols // GROUP
    part = 2 * quart * count
    size = GROUP * part
    slots = GROUP + 4
    me, mb = lax.axis_index("frame"), lax.axis_index("band")
    up, down = (mb + nb - 1) % nb, (mb + 1) % nb
    r = me % GROUP
    base = me - r
    after, before = (me + GROUP) % n, (me + n - GROUP) % n
    others = [(r + d) % GROUP for d in range(1, GROUP)]

    barrier = pltpu.get_barrier_semaphore()
    for other in (up, down):
        pl.semaphore_signal(barrier, inc=1, device_id={"band": other}, device_id_type=MESH)
    for other in [base + j for j in others] + [after, before]:
        pl.semaphore_signal(barrier, inc=1, device_id={"frame": other}, device_id_type=MESH)
    pairs = [
        (x_hbm, x_ref), (c_hbm, c_ref), (w1_hbm, w1_ref), (table_hbm, table_ref), (w2_hbm, w2_ref),
        (wq_hbm, wq_ref), (wk_hbm, wk_ref), (wv_hbm, wv_ref), (wo_hbm, wo_ref),
    ]
    loads = [pltpu.make_async_copy(s, d, load_sem.at[i]) for i, (s, d) in enumerate(pairs)]
    loads[0].start()
    loads[1].start()

    def halo(src, dst, i, other):
        return pltpu.make_async_remote_copy(
            src_ref=src, dst_ref=dst, send_sem=send_h.at[i], recv_sem=recv_h.at[i],
            device_id={"band": other}, device_id_type=MESH,
        )

    def share(j):
        return pl.ds(pl.multiple_of(j * part, part), part)

    def to_mate(k, j, slot, sem):
        return pltpu.make_async_remote_copy(
            src_ref=ready.at[k, share(j)], dst_ref=win.at[k, 2 + slot], send_sem=send_a.at[k, j],
            recv_sem=recv_a.at[k, sem], device_id={"frame": base + j}, device_id_type=MESH,
        )

    def along(k, j):
        return pltpu.make_async_remote_copy(
            src_ref=win.at[k, 2 + j], dst_ref=win.at[k, (j + 6) % 8], send_sem=send_b.at[k, j],
            recv_sem=recv_b.at[k, j], device_id={"frame": (me + GROUP * (2 * (j // 2) - 1) + n) % n},
            device_id_type=MESH,
        )

    def back_to(k, j, place, sem):
        return pltpu.make_async_remote_copy(
            src_ref=att.at[k, j], dst_ref=got.at[k, place], send_sem=send_d.at[k, j],
            recv_sem=recv_d.at[k, sem], device_id={"frame": base + j}, device_id_type=MESH,
        )

    loads[0].wait()
    loads[1].wait()
    for load in loads[2:]:
        load.start()
    merged[...] = (x_ref[...].astype(F32) + c_ref[...].astype(F32)).astype(BF16)
    pl.semaphore_wait(barrier, GROUP + 3)
    to_down = halo(merged.at[:, pl.ds(rows - 2, 2)], top, 0, down)
    to_up = halo(merged.at[:, pl.ds(0, 2)], bottom, 1, up)
    to_down.start()
    to_up.start()

    def widen(at, block):
        wide1[:, at : at + block.shape[1]] = taps(block)

    for y in range(0, rows, 2):
        widen(2 + y, merged[:, y : y + 2])

    steps = table_ref.shape[1]
    picked = (lax.broadcasted_iota(jnp.int32, (8, steps), 1) == step_ref[0]).astype(F32)
    loads[3].wait()
    embed = lax.dot_general(
        picked, table_ref[...], (((1,), (1,)), ((), ())),
        precision=lax.Precision.HIGHEST, preferred_element_type=F32,
    )[0:1]
    to = lax.broadcasted_iota(jnp.int32, (size, size), 0)
    of = lax.broadcasted_iota(jnp.int32, (size, size), 1)

    def source(i):
        quarter, y = i // part, (i // (quart * count)) % 2
        return (i % count) * (2 * cols) + y * cols + quarter * quart + (i // count) % quart

    to_pixels = (source(to) == of).astype(F32).astype(BF16)
    to_frames = (source(of) == to).astype(F32).astype(BF16)
    has_top = (mb > 0).astype(F32)
    has_bottom = (mb < nb - 1).astype(F32)
    loads[2].wait()

    def conv(wide, weight, spans):
        out = None
        for a in range(3):
            rows_in = [
                wide[:, at + a : at + a + extent].reshape(-1, 3 * chans) for at, extent in spans
            ]
            rows_in = rows_in[0] if len(spans) == 1 else jnp.concatenate(rows_in, axis=0)
            term = jnp.dot(rows_in, weight[a], preferred_element_type=F32)
            out = term if out is None else out + term
        return out

    def first_conv(spans):
        acc = conv(wide1, w1_ref, spans) + embed
        act = acc / (1.0 + jnp.exp(-acc))
        begin = 0
        for at, extent in spans:
            block = act[begin : begin + count * extent * cols]
            begin += count * extent * cols
            block = block.reshape(count, extent, cols, chans)
            row = lax.broadcasted_iota(jnp.int32, (1, extent, 1, chans), 1)
            if at == 0:
                block = block * jnp.where(row == 0, has_top, 1.0)
            if at + extent == rows + 2:
                block = block * jnp.where(row == extent - 1, has_bottom, 1.0)
            wide2[:, at : at + extent] = taps(block)

    def second_conv(spans, k):
        sums = conv(wide2, w2_ref, spans)
        begin = 0
        for at, extent in spans:
            block = sums[begin : begin + count * extent * cols]
            begin += count * extent * cols
            block = block.reshape(count, extent, cols, chans)
            for y in range(0, extent, 2):
                finish(block[:, y : y + 2].reshape(size, chans), at + y, k)
                k += 1

    def finish(summed, y, k):
        out = merged[:, y : y + 2].reshape(size, chans).astype(F32) + summed
        block_out[:, y : y + 2] = out.reshape(count, 2, cols, chans)
        centre = out - jnp.mean(out, axis=1, keepdims=True)
        scale = lax.rsqrt(jnp.mean(centre * centre, axis=1, keepdims=True) + 1e-05)
        normed = (centre * scale * gain_ref[...].reshape(1, chans)).astype(BF16)
        ready[k] = jnp.dot(to_pixels, normed, preferred_element_type=F32).astype(BF16)
        for i in others:
            to_mate(k, i, r, r).start()
        win[k, 2 + r] = ready[k, share(r)]
        along(k, r).start()

    def forward(k):
        for i in others:
            to_mate(k, i, i, i).wait_recv()
            along(k, i).start()

    order = list(range(1, chunks - 1)) + [0, chunks - 1]
    first_conv([(2, rows - 2)])
    loads[4].wait()
    second_conv([(2, rows - 4)], 0)
    to_down.wait()
    to_up.wait()
    widen(0, top[...].astype(F32) * has_top)
    widen(2 + rows, bottom[...].astype(F32) * has_bottom)
    first_conv([(0, 2), (rows, 2)])
    for k in range(chunks - 2):
        forward(k)
    second_conv([(0, 2), (rows - 2, 2)], chunks - 2)

    q = lax.broadcasted_iota(jnp.int32, (GROUP * 2 * count, slots * 2 * count), 0)
    c = lax.broadcasted_iota(jnp.int32, (GROUP * 2 * count, slots * 2 * count), 1)
    q_frame = q // (2 * count) * count + q % count
    delta = c // (2 * count) * count + c % count - 2 * count - q_frame
    total = reach_ref.shape[0]
    lane = lax.broadcasted_iota(jnp.int32, (q.shape[0], total), 1)
    q_of = lax.broadcasted_iota(jnp.int32, (q.shape[0], total), 0)
    q_of = q_of // (2 * count) * count + q_of % count + base * count
    limit = jnp.sum(
        jnp.where(lane == q_of, reach_ref[...].reshape(1, total).astype(F32), 0.0),
        axis=1, keepdims=True,
    )
    same = (q // count) % 2 == (c // count) % 2
    allowed = jnp.logical_and(jnp.abs(delta).astype(F32) <= limit, same)
    tables = [jnp.zeros(q.shape, F32) for _ in range(heads)]
    for s in range(2 * span + 1):
        hit = delta == s - span
        for h in range(heads):
            tables[h] = jnp.where(hit, rel_ref[h, s], tables[h])
    for h in range(heads):
        bias[h * q.shape[0] : (h + 1) * q.shape[0]] = jnp.where(
            allowed, tables[h] * LOG2E, -jnp.inf
        )
    forward(chunks - 2)
    forward(chunks - 1)

    for load in loads[5:]:
        load.wait()
    head_of = lax.broadcasted_iota(jnp.int32, (1, chans), 1) // (chans // heads)
    masks = [(head_of == h).astype(F32).astype(BF16) for h in range(heads)]
    scale = LOG2E * (chans // heads) ** (-0.5)
    edge = GROUP * 2 * count
    ones = jnp.ones((slots * 2 * count, slots * 2 * count), BF16)

    def attend(k, carry):
        for j in range(GROUP):
            along(k, j).wait_recv()
        field = win[k].reshape(slots * part, chans)
        keys = jnp.dot(field, wk_ref[...], preferred_element_type=F32)
        values = jnp.dot(field, wv_ref[...], preferred_element_type=F32)
        queries = jnp.dot(
            field[2 * part : (2 + GROUP) * part], wq_ref[...], preferred_element_type=F32
        )
        keys = keys.astype(BF16).reshape(slots, part, chans)
        values = values.astype(BF16).reshape(slots, part, chans)
        queries = queries.astype(BF16).reshape(GROUP, part, chans)
        for first in range(0, part, 2 * count):
            last = first + 2 * count
            qs = queries[:, first:last].reshape(edge, chans)
            ks = keys[:, first:last].reshape(slots * 2 * count, chans)
            vs = values[:, first:last].reshape(slots * 2 * count, chans)
            qx = jnp.concatenate([qs * mask for mask in masks], axis=0)
            s = lax.dot_general(qx, ks, (((1,), (1,)), ((), ())), preferred_element_type=F32)
            s = s * scale + bias[...]
            e = jnp.exp2(s - jnp.max(s, axis=1, keepdims=True))
            e = e.astype(BF16)
            w = (e.astype(F32) / jnp.dot(e, ones, preferred_element_type=F32)).astype(BF16)
            w = jnp.concatenate([w[h * edge : (h + 1) * edge] for h in range(heads)], axis=1)
            vx = jnp.concatenate([vs * mask for mask in masks], axis=0)
            o = jnp.dot(w, vx, preferred_element_type=F32).astype(BF16)
            att[k, :, first:last] = o.reshape(GROUP, 2 * count, chans)
        for j in others:
            back_to(k, j, r, r).start()
        got[k, r] = att[k, r]
        return carry

    lax.fori_loop(0, chunks, attend, 0)
    for k, y in enumerate(order):
        for j in others:
            back_to(k, j, j, j).wait_recv()
        block = got[k].reshape(size, chans)
        block = jnp.dot(to_frames, block, preferred_element_type=F32).astype(BF16)
        mixed = jnp.dot(block, wo_ref[...], preferred_element_type=F32)
        out_ref[:, 2 * y : 2 * y + 2] = block_out[:, 2 * y : 2 * y + 2] + mixed.reshape(
            count, 2, cols, chans
        )
    for k in range(chunks):
        for j in others:
            to_mate(k, j, r, r).wait_send()
            back_to(k, j, r, r).wait_send()
        for j in range(GROUP):
            along(k, j).wait_send()


def shards(
    n, nb,
    frames, control, conv_first, conv_second, time_table, step_index, norm_gain,
    w_query, w_key, w_value, w_out, rel_bias, reach,
):
    count, rows, cols, chans = frames.shape
    heads, width = rel_bias.shape
    chunks, part, slots = rows // 2, 2 * cols // GROUP * count, GROUP + 4
    table = time_table.T
    hbm = pl.BlockSpec(memory_space=pltpu.HBM)
    smem = pl.BlockSpec(memory_space=pltpu.SMEM)
    vmem = pl.BlockSpec(memory_space=pltpu.VMEM)
    wide = (3, 3 * chans, chans)
    square = pltpu.VMEM((chans, chans), BF16)
    dma = pltpu.SemaphoreType.DMA((chunks, GROUP))
    return pl.pallas_call(
        functools.partial(kernel, n, nb, heads, (width - 1) // 2),
        out_shape=jax.ShapeDtypeStruct((count, rows, cols, chans), F32),
        in_specs=[hbm] * 9 + [smem, smem, vmem, vmem],
        out_specs=vmem,
        scratch_shapes=[
            pltpu.VMEM(frames.shape, BF16),
            pltpu.VMEM(frames.shape, BF16),
            pltpu.VMEM(wide, BF16),
            pltpu.VMEM(wide, BF16),
            pltpu.VMEM(table.shape, F32),
            square, square, square, square,
            pltpu.VMEM(frames.shape, BF16),
            pltpu.VMEM((count, 2, cols, chans), BF16),
            pltpu.VMEM((count, 2, cols, chans), BF16),
            pltpu.VMEM((count, rows + 4, cols, 3 * chans), BF16),
            pltpu.VMEM((count, rows + 2, cols, 3 * chans), BF16),
            pltpu.VMEM(frames.shape, F32),
            pltpu.VMEM((chunks, GROUP * part, chans), BF16),
            pltpu.VMEM((chunks, slots, part, chans), BF16),
            pltpu.VMEM((chunks, GROUP, part, chans), BF16),
            pltpu.VMEM((chunks, GROUP, part, chans), BF16),
            pltpu.VMEM((heads * GROUP * 2 * count, slots * 2 * count), F32),
            pltpu.SemaphoreType.DMA((9,)),
            pltpu.SemaphoreType.DMA((2,)),
            pltpu.SemaphoreType.DMA((2,)),
            dma, dma, dma, dma, dma, dma,
        ],
        compiler_params=pltpu.CompilerParams(
            collective_id=0, has_side_effects=True, vmem_limit_bytes=56 * 2**20
        ),
    )(
        frames, control, conv_first.reshape(wide), conv_second.reshape(wide), table,
        w_query, w_key, w_value, w_out, step_index, rel_bias, norm_gain, reach,
    )


def solution(mesh):
    split = P("frame", "band", None, None)
    return jax.shard_map(
        functools.partial(shards, mesh.shape["frame"], mesh.shape["band"]),
        mesh=mesh,
        in_specs=(split, split) + (P(),) * 11,
        out_specs=split,
        check_vma=False,
    )
```

```python
import functools

import jax
import jax.numpy as jnp
from jax import lax
from jax.experimental import pallas as pl
from jax.experimental.pallas import tpu as pltpu
from jax.sharding import PartitionSpec as P

MESH = pl.DeviceIdType.MESH
LOG2E = 1.4426950408889634
GROUP = 4
BF16 = jnp.bfloat16
F32 = jnp.float32


def taps(block):
    shape = block.shape
    cols, chans = shape[2:]
    flat = block.astype(F32).reshape(-1, chans)
    n = flat.shape[0]
    col = lax.broadcasted_iota(jnp.int32, (1, cols, chans), 1)
    left = pltpu.roll(flat, 1, 0).reshape(-1, cols, chans) * (col > 0).astype(F32)
    right = pltpu.roll(flat, n - 1, 0).reshape(-1, cols, chans) * (col < cols - 1).astype(F32)
    sides = [left.astype(BF16), flat.astype(BF16).reshape(-1, cols, chans), right.astype(BF16)]
    return jnp.concatenate(sides, axis=-1).reshape(shape[:3] + (3 * chans,))


def kernel(
    n, nb, heads, span,
    x_hbm, c_hbm, w1_hbm, w2_hbm, table_hbm, wq_hbm, wk_hbm, wv_hbm, wo_hbm,
    step_ref, rel_ref, gain_ref, reach_ref,
    out_ref,
    x_ref, c_ref, w1_ref, w2_ref, table_ref, wq_ref, wk_ref, wv_ref, wo_ref,
    merged, top, bottom, wide1, wide2, block_out, ready, win, att, got, bias, load_sem,
    send_h, recv_h, send_a, recv_a, send_b, recv_b, send_d, recv_d,
):
    count, rows, cols, chans = x_ref.shape
    chunks = rows // 2
    quart = cols // GROUP
    part = 2 * quart * count
    size = GROUP * part
    slots = GROUP + 4
    me, mb = lax.axis_index("frame"), lax.axis_index("band")
    up, down = (mb + nb - 1) % nb, (mb + 1) % nb
    r = me % GROUP
    base = me - r
    after, before = (me + GROUP) % n, (me + n - GROUP) % n
    others = [(r + d) % GROUP for d in range(1, GROUP)]

    barrier = pltpu.get_barrier_semaphore()
    for other in (up, down):
        pl.semaphore_signal(barrier, inc=1, device_id={"band": other}, device_id_type=MESH)
    for other in [base + j for j in others] + [after, before]:
        pl.semaphore_signal(barrier, inc=1, device_id={"frame": other}, device_id_type=MESH)
    pairs = [
        (x_hbm, x_ref), (c_hbm, c_ref), (w1_hbm, w1_ref), (table_hbm, table_ref), (w2_hbm, w2_ref),
        (wq_hbm, wq_ref), (wk_hbm, wk_ref), (wv_hbm, wv_ref), (wo_hbm, wo_ref),
    ]
    loads = [pltpu.make_async_copy(s, d, load_sem.at[i]) for i, (s, d) in enumerate(pairs)]
    loads[0].start()
    loads[1].start()

    def halo(src, dst, i, other):
        return pltpu.make_async_remote_copy(
            src_ref=src, dst_ref=dst, send_sem=send_h.at[i], recv_sem=recv_h.at[i],
            device_id={"band": other}, device_id_type=MESH,
        )

    def share(j):
        return pl.ds(pl.multiple_of(j * part, part), part)

    def to_mate(k, j, slot, sem):
        return pltpu.make_async_remote_copy(
            src_ref=ready.at[k, share(j)], dst_ref=win.at[k, 2 + slot], send_sem=send_a.at[k, j],
            recv_sem=recv_a.at[k, sem], device_id={"frame": base + j}, device_id_type=MESH,
        )

    def along(k, j):
        return pltpu.make_async_remote_copy(
            src_ref=win.at[k, 2 + j], dst_ref=win.at[k, (j + 6) % 8], send_sem=send_b.at[k, j],
            recv_sem=recv_b.at[k, j], device_id={"frame": (me + GROUP * (2 * (j // 2) - 1) + n) % n},
            device_id_type=MESH,
        )

    def back_to(k, j, place, sem):
        return pltpu.make_async_remote_copy(
            src_ref=att.at[k, j], dst_ref=got.at[k, place], send_sem=send_d.at[k, j],
            recv_sem=recv_d.at[k, sem], device_id={"frame": base + j}, device_id_type=MESH,
        )

    loads[0].wait()
    loads[1].wait()
    for load in loads[2:]:
        load.start()
    merged[...] = (x_ref[...].astype(F32) + c_ref[...].astype(F32)).astype(BF16)
    pl.semaphore_wait(barrier, GROUP + 3)
    to_down = halo(merged.at[:, pl.ds(rows - 2, 2)], top, 0, down)
    to_up = halo(merged.at[:, pl.ds(0, 2)], bottom, 1, up)
    to_down.start()
    to_up.start()

    def widen(at, block):
        wide1[:, at : at + block.shape[1]] = taps(block)

    for y in range(0, rows, 2):
        widen(2 + y, merged[:, y : y + 2])

    steps = table_ref.shape[1]
    picked = (lax.broadcasted_iota(jnp.int32, (8, steps), 1) == step_ref[0]).astype(F32)
    loads[3].wait()
    embed = lax.dot_general(
        picked, table_ref[...], (((1,), (1,)), ((), ())),
        precision=lax.Precision.HIGHEST, preferred_element_type=F32,
    )[0:1]
    to = lax.broadcasted_iota(jnp.int32, (size, size), 0)
    of = lax.broadcasted_iota(jnp.int32, (size, size), 1)

    def source(i):
        quarter, y = i // part, (i // (quart * count)) % 2
        return (i % count) * (2 * cols) + y * cols + quarter * quart + (i // count) % quart

    to_pixels = (source(to) == of).astype(F32).astype(BF16)
    to_frames = (source(of) == to).astype(F32).astype(BF16)
    has_top = (mb > 0).astype(F32)
    has_bottom = (mb < nb - 1).astype(F32)
    loads[2].wait()

    def first_conv(m):
        acc = embed
        for a in range(3):
            acc = acc + jnp.dot(
                wide1[:, 2 * m + a : 2 * m + a + 2].reshape(size, 3 * chans), w1_ref[a],
                preferred_element_type=F32,
            )
        act = acc / (1.0 + jnp.exp(-acc))
        act = act.reshape(count, 2, cols, chans)
        row = lax.broadcasted_iota(jnp.int32, (1, 2, 1, chans), 1)
        if m == 0:
            act = act * jnp.where(row == 0, has_top, 1.0)
        if m == chunks:
            act = act * jnp.where(row == 1, has_bottom, 1.0)
        wide2[:, 2 * m : 2 * m + 2] = taps(act)

    def second_conv(j, k):
        out = merged[:, 2 * j : 2 * j + 2].reshape(size, chans).astype(F32)
        conv = None
        for a in range(3):
            part_sum = jnp.dot(
                wide2[:, 2 * j + a : 2 * j + a + 2].reshape(size, 3 * chans), w2_ref[a],
                preferred_element_type=F32,
            )
            conv = part_sum if conv is None else conv + part_sum
        out = out + conv
        block_out[:, 2 * j : 2 * j + 2] = out.reshape(count, 2, cols, chans)
        centre = out - jnp.mean(out, axis=1, keepdims=True)
        scale = lax.rsqrt(jnp.mean(centre * centre, axis=1, keepdims=True) + 1e-05)
        normed = (centre * scale * gain_ref[...].reshape(1, chans)).astype(BF16)
        ready[k] = jnp.dot(to_pixels, normed, preferred_element_type=F32).astype(BF16)
        for i in others:
            to_mate(k, i, r, r).start()
        win[k, 2 + r] = ready[k, share(r)]
        along(k, r).start()

    def forward(k):
        for i in others:
            to_mate(k, i, i, i).wait_recv()
            along(k, i).start()

    order = list(range(1, chunks - 1)) + [0, chunks - 1]
    first_conv(1)
    for k, j in enumerate(order):
        if j == 0:
            to_down.wait()
            to_up.wait()
            widen(0, top[...].astype(F32) * has_top)
            widen(2 + rows, bottom[...].astype(F32) * has_bottom)
            first_conv(0)
        else:
            first_conv(j + 1)
        if k == 0:
            loads[4].wait()
        second_conv(j, k)
        if k > 0:
            forward(k - 1)

    held, seen = GROUP * count, slots * count
    q = lax.broadcasted_iota(jnp.int32, (held, 2 * seen), 0)
    c = lax.broadcasted_iota(jnp.int32, (held, 2 * seen), 1)
    delta = c % seen - 2 * count - q
    total = reach_ref.shape[0]
    lane = lax.broadcasted_iota(jnp.int32, (held, total), 1)
    q_of = lax.broadcasted_iota(jnp.int32, (held, total), 0) + base * count
    limit = jnp.sum(
        jnp.where(lane == q_of, reach_ref[...].reshape(1, total).astype(F32), 0.0),
        axis=1, keepdims=True,
    )
    allowed = jnp.abs(delta).astype(F32) <= limit
    first_half = c < seen
    tables = [jnp.zeros(q.shape, F32) for _ in range(heads // 2)]
    for s in range(2 * span + 1):
        hit = delta == s - span
        for g in range(heads // 2):
            both = jnp.where(first_half, rel_ref[2 * g, s], rel_ref[2 * g + 1, s])
            tables[g] = jnp.where(hit, both, tables[g])
    for g in range(heads // 2):
        bias[g * held : (g + 1) * held] = jnp.where(allowed, tables[g] * LOG2E, -jnp.inf)
    forward(chunks - 1)

    for load in loads[5:]:
        load.wait()
    head_of = lax.broadcasted_iota(jnp.int32, (1, chans), 1) // (chans // heads)
    pair_masks = [(head_of // 2 == g).astype(F32) for g in range(heads // 2)]
    pair_bf16 = [mask.astype(BF16) for mask in pair_masks]
    halves = [(head_of % 2 == i).astype(F32).astype(BF16) for i in range(2)]
    scale = LOG2E * (chans // heads) ** (-0.5)
    own = lax.broadcasted_iota(jnp.int32, (2 * seen, 2 * seen), 0) // seen
    own = own == lax.broadcasted_iota(jnp.int32, (2 * seen, 2 * seen), 1) // seen
    ones = own.astype(F32).astype(BF16)
    left = lax.broadcasted_iota(jnp.int32, (heads // 2 * held, 2 * seen), 1) < seen

    def attend(k, carry):
        for j in range(GROUP):
            along(k, j).wait_recv()
        field = win[k].reshape(slots * part, chans)
        pixels = part // count
        keys = jnp.dot(field, wk_ref[...], preferred_element_type=F32)
        values = jnp.dot(field, wv_ref[...], preferred_element_type=F32)
        queries = jnp.dot(
            field[2 * part : (2 + GROUP) * part], wq_ref[...], preferred_element_type=F32
        )
        keys = keys.reshape(slots, pixels, count, chans)
        values = values.reshape(slots, pixels, count, chans)
        queries = queries.reshape(GROUP, pixels, count, chans)
        done = []
        for p in range(pixels):
            qs = queries[:, p].reshape(held, chans).astype(BF16)
            ks = keys[:, p].reshape(seen, chans).astype(BF16)
            vs = values[:, p].reshape(seen, chans).astype(BF16)
            qx = jnp.concatenate([qs * mask for mask in pair_bf16], axis=0)
            kx = jnp.concatenate([ks * mask for mask in halves], axis=0)
            vx = jnp.concatenate([vs * mask for mask in halves], axis=0)
            s = lax.dot_general(qx, kx, (((1,), (1,)), ((), ())), preferred_element_type=F32)
            s = s * scale + bias[...]
            top_left = jnp.max(jnp.where(left, s, -jnp.inf), axis=1, keepdims=True)
            top_right = jnp.max(jnp.where(left, -jnp.inf, s), axis=1, keepdims=True)
            e = jnp.exp2(s - jnp.where(left, top_left, top_right)).astype(BF16)
            w = (e.astype(F32) / jnp.dot(e, ones, preferred_element_type=F32)).astype(BF16)
            o = jnp.dot(w, vx, preferred_element_type=F32)
            o = sum(o[g * held : (g + 1) * held] * pair_masks[g] for g in range(heads // 2))
            done.append(o.reshape(GROUP, count, chans))
            if len(done) == 2:
                first = (p - 1) * count
                att[k, :, first : first + 2 * count] = jnp.concatenate(done, axis=1).astype(BF16)
                done = []
        for j in others:
            back_to(k, j, r, r).start()
        got[k, r] = att[k, r]
        return carry

    lax.fori_loop(0, chunks, attend, 0)
    for k, y in enumerate(order):
        for j in others:
            back_to(k, j, j, j).wait_recv()
        block = got[k].reshape(size, chans)
        block = jnp.dot(to_frames, block, preferred_element_type=F32).astype(BF16)
        mixed = jnp.dot(block, wo_ref[...], preferred_element_type=F32)
        out_ref[:, 2 * y : 2 * y + 2] = block_out[:, 2 * y : 2 * y + 2] + mixed.reshape(
            count, 2, cols, chans
        )
    for k in range(chunks):
        for j in others:
            to_mate(k, j, r, r).wait_send()
            back_to(k, j, r, r).wait_send()
        for j in range(GROUP):
            along(k, j).wait_send()


def shards(
    n, nb,
    frames, control, conv_first, conv_second, time_table, step_index, norm_gain,
    w_query, w_key, w_value, w_out, rel_bias, reach,
):
    count, rows, cols, chans = frames.shape
    heads, width = rel_bias.shape
    chunks, part, slots = rows // 2, 2 * cols // GROUP * count, GROUP + 4
    table = time_table.T
    hbm = pl.BlockSpec(memory_space=pltpu.HBM)
    smem = pl.BlockSpec(memory_space=pltpu.SMEM)
    vmem = pl.BlockSpec(memory_space=pltpu.VMEM)
    wide = (3, 3 * chans, chans)
    square = pltpu.VMEM((chans, chans), BF16)
    dma = pltpu.SemaphoreType.DMA((chunks, GROUP))
    return pl.pallas_call(
        functools.partial(kernel, n, nb, heads, (width - 1) // 2),
        out_shape=jax.ShapeDtypeStruct((count, rows, cols, chans), F32),
        in_specs=[hbm] * 9 + [smem, smem, vmem, vmem],
        out_specs=vmem,
        scratch_shapes=[
            pltpu.VMEM(frames.shape, BF16),
            pltpu.VMEM(frames.shape, BF16),
            pltpu.VMEM(wide, BF16),
            pltpu.VMEM(wide, BF16),
            pltpu.VMEM(table.shape, F32),
            square, square, square, square,
            pltpu.VMEM(frames.shape, BF16),
            pltpu.VMEM((count, 2, cols, chans), BF16),
            pltpu.VMEM((count, 2, cols, chans), BF16),
            pltpu.VMEM((count, rows + 4, cols, 3 * chans), BF16),
            pltpu.VMEM((count, rows + 2, cols, 3 * chans), BF16),
            pltpu.VMEM(frames.shape, F32),
            pltpu.VMEM((chunks, GROUP * part, chans), BF16),
            pltpu.VMEM((chunks, slots, part, chans), BF16),
            pltpu.VMEM((chunks, GROUP, part, chans), BF16),
            pltpu.VMEM((chunks, GROUP, part, chans), BF16),
            pltpu.VMEM((heads // 2 * GROUP * count, 2 * slots * count), F32),
            pltpu.SemaphoreType.DMA((9,)),
            pltpu.SemaphoreType.DMA((2,)),
            pltpu.SemaphoreType.DMA((2,)),
            dma, dma, dma, dma, dma, dma,
        ],
        compiler_params=pltpu.CompilerParams(
            collective_id=0, has_side_effects=True, vmem_limit_bytes=56 * 2**20
        ),
    )(
        frames, control, conv_first.reshape(wide), conv_second.reshape(wide), table,
        w_query, w_key, w_value, w_out, step_index, rel_bias, norm_gain, reach,
    )


def solution(mesh):
    split = P("frame", "band", None, None)
    return jax.shard_map(
        functools.partial(shards, mesh.shape["frame"], mesh.shape["band"]),
        mesh=mesh,
        in_specs=(split, split) + (P(),) * 11,
        out_specs=split,
        check_vma=False,
    )
```

```python
import functools

import jax
import jax.numpy as jnp
from jax import lax
from jax.experimental import pallas as pl
from jax.experimental.pallas import tpu as pltpu
from jax.sharding import PartitionSpec as P

MESH = pl.DeviceIdType.MESH
LOG2E = 1.4426950408889634
GROUP = 4
BF16 = jnp.bfloat16
F32 = jnp.float32


def taps(flat, cols):
    n = flat.shape[0]
    col = lax.broadcasted_iota(jnp.int32, flat.shape, 0) % cols
    left = jnp.where(col == 0, 0.0, pltpu.roll(flat, 1, 0))
    right = jnp.where(col == cols - 1, 0.0, pltpu.roll(flat, n - 1, 0))
    return jnp.concatenate([left.astype(BF16), flat.astype(BF16), right.astype(BF16)], axis=-1)


def kernel(
    n, nb, heads, span,
    x_hbm, c_hbm, w1_hbm, w2_hbm, table_hbm, wq_hbm, wk_hbm, wv_hbm, wo_hbm,
    step_ref, rel_ref, gain_ref, reach_ref,
    out_ref,
    x_ref, c_ref, w1_ref, w2_ref, table_ref, wq_ref, wk_ref, wv_ref, wo_ref,
    merged, top, bottom, wide1, wide2, block_out, ready, win, att, got, bias, load_sem,
    send_h, recv_h, send_a, recv_a, send_b, recv_b, send_d, recv_d,
):
    count, rows, cols, chans = x_ref.shape
    chunks = rows // 2
    quart = cols // GROUP
    part = 2 * quart * count
    size = GROUP * part
    slots = GROUP + 4
    me, mb = lax.axis_index("frame"), lax.axis_index("band")
    up, down = (mb + nb - 1) % nb, (mb + 1) % nb
    r = me % GROUP
    base = me - r
    after, before = (me + GROUP) % n, (me + n - GROUP) % n
    others = [(r + d) % GROUP for d in range(1, GROUP)]

    barrier = pltpu.get_barrier_semaphore()
    for other in (up, down):
        pl.semaphore_signal(barrier, inc=1, device_id={"band": other}, device_id_type=MESH)
    for other in [base + j for j in others] + [after, before]:
        pl.semaphore_signal(barrier, inc=1, device_id={"frame": other}, device_id_type=MESH)
    pairs = [
        (x_hbm, x_ref), (c_hbm, c_ref), (w1_hbm, w1_ref), (table_hbm, table_ref), (w2_hbm, w2_ref),
        (wq_hbm, wq_ref), (wk_hbm, wk_ref), (wv_hbm, wv_ref), (wo_hbm, wo_ref),
    ]
    loads = [pltpu.make_async_copy(s, d, load_sem.at[i]) for i, (s, d) in enumerate(pairs)]
    for load in loads:
        load.start()

    def halo(src, dst, i, other):
        return pltpu.make_async_remote_copy(
            src_ref=src, dst_ref=dst, send_sem=send_h.at[i], recv_sem=recv_h.at[i],
            device_id={"band": other}, device_id_type=MESH,
        )

    def share(j):
        return pl.ds(pl.multiple_of(j * part, part), part)

    def to_mate(k, j, slot, sem):
        return pltpu.make_async_remote_copy(
            src_ref=ready.at[k, share(j)], dst_ref=win.at[k, 2 + slot], send_sem=send_a.at[k, j],
            recv_sem=recv_a.at[k, sem], device_id={"frame": base + j}, device_id_type=MESH,
        )

    def along(k, j):
        return pltpu.make_async_remote_copy(
            src_ref=win.at[k, 2 + j], dst_ref=win.at[k, (j + 6) % 8], send_sem=send_b.at[k, j],
            recv_sem=recv_b.at[k, j], device_id={"frame": (me + GROUP * (2 * (j // 2) - 1) + n) % n},
            device_id_type=MESH,
        )

    def back_to(k, j, place, sem):
        return pltpu.make_async_remote_copy(
            src_ref=att.at[k, j], dst_ref=got.at[k, place], send_sem=send_d.at[k, j],
            recv_sem=recv_d.at[k, sem], device_id={"frame": base + j}, device_id_type=MESH,
        )

    loads[0].wait()
    loads[1].wait()
    merged[...] = (x_ref[...].astype(F32) + c_ref[...].astype(F32)).astype(BF16)
    pl.semaphore_wait(barrier, GROUP + 3)
    to_down = halo(merged.at[:, pl.ds(rows - 2, 2)], top, 0, down)
    to_up = halo(merged.at[:, pl.ds(0, 2)], bottom, 1, up)
    to_down.start()
    to_up.start()

    def widen(at, block):
        flat = block.astype(F32).reshape(-1, chans)
        wide1[:, at : at + block.shape[1]] = taps(flat, cols).reshape(block.shape[:3] + (3 * chans,))

    for y in range(0, rows, 2):
        widen(2 + y, merged[:, y : y + 2])

    steps = table_ref.shape[1]
    picked = (lax.broadcasted_iota(jnp.int32, (8, steps), 1) == step_ref[0]).astype(F32)
    loads[3].wait()
    embed = lax.dot_general(
        picked, table_ref[...], (((1,), (1,)), ((), ())),
        precision=lax.Precision.HIGHEST, preferred_element_type=F32,
    )[0:1]
    to = lax.broadcasted_iota(jnp.int32, (size, size), 0)
    of = lax.broadcasted_iota(jnp.int32, (size, size), 1)

    def source(i):
        quarter, y = i // part, (i // (quart * count)) % 2
        return (i % count) * (2 * cols) + y * cols + quarter * quart + (i // count) % quart

    to_pixels = (source(to) == of).astype(F32).astype(BF16)
    to_frames = (source(of) == to).astype(F32).astype(BF16)
    has_top = (mb > 0).astype(F32)
    has_bottom = (mb < nb - 1).astype(F32)
    loads[2].wait()

    def first_conv(m):
        acc = embed
        for a in range(3):
            acc = acc + jnp.dot(
                wide1[:, 2 * m + a : 2 * m + a + 2].reshape(size, 3 * chans), w1_ref[a],
                preferred_element_type=F32,
            )
        act = acc / (1.0 + jnp.exp(-acc))
        row = (lax.broadcasted_iota(jnp.int32, act.shape, 0) // cols) % 2
        if m == 0:
            act = act * jnp.where(row == 0, has_top, 1.0)
        if m == chunks:
            act = act * jnp.where(row == 1, has_bottom, 1.0)
        wide2[:, 2 * m : 2 * m + 2] = taps(act, cols).reshape(count, 2, cols, 3 * chans)

    def second_conv(j, k):
        out = merged[:, 2 * j : 2 * j + 2].reshape(size, chans).astype(F32)
        conv = None
        for a in range(3):
            part_sum = jnp.dot(
                wide2[:, 2 * j + a : 2 * j + a + 2].reshape(size, 3 * chans), w2_ref[a],
                preferred_element_type=F32,
            )
            conv = part_sum if conv is None else conv + part_sum
        out = out + conv
        block_out[:, 2 * j : 2 * j + 2] = out.reshape(count, 2, cols, chans)
        centre = out - jnp.mean(out, axis=1, keepdims=True)
        scale = lax.rsqrt(jnp.mean(centre * centre, axis=1, keepdims=True) + 1e-05)
        normed = (centre * scale * gain_ref[...].reshape(1, chans)).astype(BF16)
        ready[k] = jnp.dot(to_pixels, normed, preferred_element_type=F32).astype(BF16)
        for i in others:
            to_mate(k, i, r, r).start()
        win[k, 2 + r] = ready[k, share(r)]
        along(k, r).start()

    def forward(k):
        for i in others:
            to_mate(k, i, i, i).wait_recv()
            along(k, i).start()

    order = list(range(1, chunks - 1)) + [0, chunks - 1]
    first_conv(1)
    for k, j in enumerate(order):
        if j == 0:
            to_down.wait()
            to_up.wait()
            widen(0, top[...].astype(F32) * has_top)
            widen(2 + rows, bottom[...].astype(F32) * has_bottom)
            first_conv(0)
        else:
            first_conv(j + 1)
        if k == 0:
            loads[4].wait()
        second_conv(j, k)
        if k > 0:
            forward(k - 1)

    held, seen = GROUP * count, slots * count
    q = lax.broadcasted_iota(jnp.int32, (held, 2 * seen), 0)
    c = lax.broadcasted_iota(jnp.int32, (held, 2 * seen), 1)
    delta = c % seen - 2 * count - q
    total = reach_ref.shape[0]
    lane = lax.broadcasted_iota(jnp.int32, (held, total), 1)
    q_of = lax.broadcasted_iota(jnp.int32, (held, total), 0) + base * count
    limit = jnp.sum(
        jnp.where(lane == q_of, reach_ref[...].reshape(1, total).astype(F32), 0.0),
        axis=1, keepdims=True,
    )
    allowed = jnp.abs(delta).astype(F32) <= limit
    first_half = c < seen
    tables = [jnp.zeros(q.shape, F32) for _ in range(heads // 2)]
    for s in range(2 * span + 1):
        hit = delta == s - span
        for g in range(heads // 2):
            both = jnp.where(first_half, rel_ref[2 * g, s], rel_ref[2 * g + 1, s])
            tables[g] = jnp.where(hit, both, tables[g])
    for g in range(heads // 2):
        bias[g * held : (g + 1) * held] = jnp.where(allowed, tables[g] * LOG2E, -jnp.inf)
    forward(chunks - 1)

    for load in loads[5:]:
        load.wait()
    head_of = lax.broadcasted_iota(jnp.int32, (1, chans), 1) // (chans // heads)
    pair_masks = [(head_of // 2 == g).astype(F32) for g in range(heads // 2)]
    pair_bf16 = [mask.astype(BF16) for mask in pair_masks]
    halves = [(head_of % 2 == i).astype(F32).astype(BF16) for i in range(2)]
    scale = LOG2E * (chans // heads) ** (-0.5)
    own = lax.broadcasted_iota(jnp.int32, (2 * seen, 2 * seen), 0) // seen
    own = own == lax.broadcasted_iota(jnp.int32, (2 * seen, 2 * seen), 1) // seen
    ones = own.astype(F32).astype(BF16)
    left = lax.broadcasted_iota(jnp.int32, (part // count * (heads // 2) * held, 2 * seen), 1) < seen

    def attend(k, carry):
        for j in range(GROUP):
            along(k, j).wait_recv()
        field = win[k].reshape(slots * part, chans)
        pixels = part // count
        keys = jnp.dot(field, wk_ref[...], preferred_element_type=F32)
        values = jnp.dot(field, wv_ref[...], preferred_element_type=F32)
        queries = jnp.dot(
            field[2 * part : (2 + GROUP) * part], wq_ref[...], preferred_element_type=F32
        )
        keys = keys.reshape(slots, pixels, count, chans)
        values = values.reshape(slots, pixels, count, chans)
        queries = queries.reshape(GROUP, pixels, count, chans)
        edge = heads // 2 * held
        scores = []
        for p in range(pixels):
            qs = queries[:, p].reshape(held, chans).astype(BF16)
            ks = keys[:, p].reshape(seen, chans).astype(BF16)
            qx = jnp.concatenate([qs * mask for mask in pair_bf16], axis=0)
            kx = jnp.concatenate([ks * mask for mask in halves], axis=0)
            scores.append(
                lax.dot_general(qx, kx, (((1,), (1,)), ((), ())), preferred_element_type=F32)
                * scale + bias[...]
            )
        s = jnp.concatenate(scores, axis=0)
        top_left = jnp.max(jnp.where(left, s, -jnp.inf), axis=1, keepdims=True)
        top_right = jnp.max(jnp.where(left, -jnp.inf, s), axis=1, keepdims=True)
        e = jnp.exp2(s - jnp.where(left, top_left, top_right)).astype(BF16)
        w = (e.astype(F32) / jnp.dot(e, ones, preferred_element_type=F32)).astype(BF16)
        mixed = []
        for p in range(pixels):
            vs = values[:, p].reshape(seen, chans).astype(BF16)
            vx = jnp.concatenate([vs * mask for mask in halves], axis=0)
            mixed.append(
                jnp.dot(w[p * edge : (p + 1) * edge], vx, preferred_element_type=F32)
            )
        mixed = [
            sum(o[g * held : (g + 1) * held] * pair_masks[g] for g in range(heads // 2)).reshape(
                GROUP, count, chans
            )
            for o in mixed
        ]
        for p in range(0, pixels, 2):
            att[k, :, p * count : (p + 2) * count] = jnp.concatenate(
                mixed[p : p + 2], axis=1
            ).astype(BF16)
        for j in others:
            back_to(k, j, r, r).start()
        got[k, r] = att[k, r]
        return carry

    lax.fori_loop(0, chunks, attend, 0)
    for k, y in enumerate(order):
        for j in others:
            back_to(k, j, j, j).wait_recv()
        block = got[k].reshape(size, chans)
        block = jnp.dot(to_frames, block, preferred_element_type=F32).astype(BF16)
        mixed = jnp.dot(block, wo_ref[...], preferred_element_type=F32)
        out_ref[:, 2 * y : 2 * y + 2] = block_out[:, 2 * y : 2 * y + 2] + mixed.reshape(
            count, 2, cols, chans
        )
    for k in range(chunks):
        for j in others:
            to_mate(k, j, r, r).wait_send()
            back_to(k, j, r, r).wait_send()
        for j in range(GROUP):
            along(k, j).wait_send()


def shards(
    n, nb,
    frames, control, conv_first, conv_second, time_table, step_index, norm_gain,
    w_query, w_key, w_value, w_out, rel_bias, reach,
):
    count, rows, cols, chans = frames.shape
    heads, width = rel_bias.shape
    chunks, part, slots = rows // 2, 2 * cols // GROUP * count, GROUP + 4
    table = time_table.T
    hbm = pl.BlockSpec(memory_space=pltpu.HBM)
    smem = pl.BlockSpec(memory_space=pltpu.SMEM)
    vmem = pl.BlockSpec(memory_space=pltpu.VMEM)
    wide = (3, 3 * chans, chans)
    square = pltpu.VMEM((chans, chans), BF16)
    dma = pltpu.SemaphoreType.DMA((chunks, GROUP))
    return pl.pallas_call(
        functools.partial(kernel, n, nb, heads, (width - 1) // 2),
        out_shape=jax.ShapeDtypeStruct((count, rows, cols, chans), F32),
        in_specs=[hbm] * 9 + [smem, smem, vmem, vmem],
        out_specs=vmem,
        scratch_shapes=[
            pltpu.VMEM(frames.shape, BF16),
            pltpu.VMEM(frames.shape, BF16),
            pltpu.VMEM(wide, BF16),
            pltpu.VMEM(wide, BF16),
            pltpu.VMEM(table.shape, F32),
            square, square, square, square,
            pltpu.VMEM(frames.shape, BF16),
            pltpu.VMEM((count, 2, cols, chans), BF16),
            pltpu.VMEM((count, 2, cols, chans), BF16),
            pltpu.VMEM((count, rows + 4, cols, 3 * chans), BF16),
            pltpu.VMEM((count, rows + 2, cols, 3 * chans), BF16),
            pltpu.VMEM(frames.shape, F32),
            pltpu.VMEM((chunks, GROUP * part, chans), BF16),
            pltpu.VMEM((chunks, slots, part, chans), BF16),
            pltpu.VMEM((chunks, GROUP, part, chans), BF16),
            pltpu.VMEM((chunks, GROUP, part, chans), BF16),
            pltpu.VMEM((heads // 2 * GROUP * count, 2 * slots * count), F32),
            pltpu.SemaphoreType.DMA((9,)),
            pltpu.SemaphoreType.DMA((2,)),
            pltpu.SemaphoreType.DMA((2,)),
            dma, dma, dma, dma, dma, dma,
        ],
        compiler_params=pltpu.CompilerParams(
            collective_id=0, has_side_effects=True, vmem_limit_bytes=56 * 2**20
        ),
    )(
        frames, control, conv_first.reshape(wide), conv_second.reshape(wide), table,
        w_query, w_key, w_value, w_out, step_index, rel_bias, norm_gain, reach,
    )


def solution(mesh):
    split = P("frame", "band", None, None)
    return jax.shard_map(
        functools.partial(shards, mesh.shape["frame"], mesh.shape["band"]),
        mesh=mesh,
        in_specs=(split, split) + (P(),) * 11,
        out_specs=split,
        check_vma=False,
    )
```
